256 devices in a mesh: sec: 16 (over y, x), bond: 16 (over z, core).
Axes of the slice: x: 4, y: 4, z: 8, core: 2. Of those that a mesh axis runs over, the one named last changes fastest.
Arguments:
- left_vectors: bfloat16 [128, 4096], P(None, 'bond'), may hold values from -6 to 6
- site_tensors: bfloat16 [16, 4096, 4, 4096], P('sec', None, None, 'bond'), may hold values from -0.09375 to 0.09375
- displacement: float32 [128, 216], P('sec'), may hold values from -2.5 to 2.5
- photon_counts: int32 [128, 216], P('sec'), may hold values from 0 to 3
- mode_order: int32 [216], replicated, may hold values from 0 to 215, each once
Outputs:
- log_likelihood: float32 [16, 128], P('sec')
- log_norm: float32 [16, 128], P('sec')
The draws below stay inside these ranges and needn't reach their ends.
Inputs may be any that keep to these rules, and one draw needn't show every extreme that they name: `mode_order`: each of the 216 modes appears once.
All inputs are finite; a program needn't handle non-finite values.
Results may differ from the reference program's by a relative error of at most 0.0015.
Values may be sent and summed in bfloat16 or wider, within the bound.
A program may use at most 64 MiB of HBM per device.

```python
import math
import jax
import jax.numpy as jnp
from jax import lax

CHI = 4096
CUT = 4
MODE_POOL = 216
SAMPLES = 128
MODES = 16


def with_ends(result, own_key, smallest, top_value):
    index_at = [jax.random.randint(jax.random.fold_in(own_key, axis), (), 0, length) for axis, length in enumerate(result.shape)]
    longest = result.shape.index(max(result.shape))
    neighbour = index_at[:longest] + [(index_at[longest] + 1) % result.shape[longest]] + index_at[longest + 1:]
    return result.at[tuple(index_at)].set(smallest).at[tuple(neighbour)].set(top_value)


def block_scale(stream_key, shape, split, low, largest):
    def one(position, shards_of):
        draws = jax.random.uniform(jax.random.fold_in(jax.random.fold_in(stream_key, 6), position), (shards_of,), jnp.float32, low / len(split), largest / len(split))
        return jnp.repeat(jnp.exp(draws), shape[position] // shards_of).reshape((-1,) + (1,) * (len(shape) - position - 1))

    level = one(*split[0])
    for cut in split[1:]:
        level = level * one(*cut)
    return level


def centred(stream_key, shape, width, reach, split=(), held_as=jnp.bfloat16):
    drawn = jax.random.normal(stream_key, shape, jnp.float32) * width
    if len(split) > 0:
        drawn = block_scale(stream_key, shape, split, -0.22, 0.18) * drawn
    return jnp.clip(drawn, min=-reach, max=reach).astype(held_as)


def setup_inputs(seed: int = 0) -> dict:
    splits = jax.random.split(jax.random.key(seed), 6)
    left_vectors = centred(splits[0], (SAMPLES, CHI), 1.0, 6.0, ((1, 16),))
    site_tensors = centred(splits[1], (MODES, CHI, CUT, CHI), CHI ** -0.5, 0.09375, ((0, 16), (3, 16)))
    displacement = centred(splits[2], (SAMPLES, MODE_POOL), 0.7, 2.5, ((0, 16),), jnp.float32)
    photon_counts = with_ends(jax.random.randint(splits[3], (SAMPLES, MODE_POOL), 0, CUT), jax.random.fold_in(splits[3], 1), 0, CUT - 1).astype(jnp.int32)
    mode_order = jax.random.permutation(splits[4], MODE_POOL).astype(jnp.int32)
    return {"left_vectors": left_vectors, "site_tensors": site_tensors, "displacement": displacement, "photon_counts": photon_counts, "mode_order": mode_order}


epsilon = 1e-06

def displacement_table(cutoff):
    table = [[[0.0 for degree_slot in range(2 * cutoff - 1)] for col_level in range(cutoff)] for row_level in range(cutoff)]
    for row_level in range(cutoff):
        for col_level in range(cutoff):
            lower = min(row_level, col_level)
            upper = max(row_level, col_level)
            excess = upper - lower
            parity = 1.0 if row_level >= col_level else (-1.0) ** excess
            prefactor = math.sqrt(math.factorial(lower) / math.factorial(upper))
            for term in range(lower + 1):
                table[row_level][col_level][excess + 2 * term] += parity * prefactor * (-1.0) ** term * math.comb(upper, lower - term) / math.factorial(term)
    return table

def displacement_matrix(amplitude):
    table = jnp.asarray(displacement_table(CUT), dtype=jnp.float32)
    power_list = [jnp.ones_like(amplitude)]
    for degree in range(2 * CUT - 2):
        power_list.append(power_list[-1] * amplitude)
    power_stack = jnp.stack(power_list, axis=1)
    poly = jnp.einsum('sp,mnp->smn', power_stack, table, precision=lax.Precision.HIGHEST)
    return jnp.exp(-0.5 * amplitude * amplitude)[:, None, None] * poly

def reference(left_vectors, site_tensors, displacement, photon_counts, mode_order):
    vectors = left_vectors
    factor = jnp.ones((left_vectors.shape[0],), jnp.float32)
    levels = jnp.arange(CUT).astype(jnp.float32)
    results = []
    norms = []
    for segment_index in range(MODES):
        column = mode_order[segment_index]
        amplitude = jnp.take(displacement, column, axis=1)
        counted = jnp.take(photon_counts, column, axis=1).astype(jnp.float32)
        matrix = site_tensors[segment_index].reshape(CHI, CUT * CHI)
        projected = jnp.dot(vectors, matrix, preferred_element_type=jnp.float32) * factor[:, None]
        projected = projected.reshape(-1, CUT, CHI)
        shifts = displacement_matrix(amplitude)
        displaced = jnp.einsum('smn,snb->smb', shifts, projected, precision=lax.Precision.HIGHEST)
        weights = lax.optimization_barrier(jnp.sum(displaced * displaced, axis=2))
        select = (counted[:, None] == levels[None, :]).astype(jnp.float32)
        chosen_weight = lax.optimization_barrier(jnp.sum(select * weights, axis=1))
        results.append(jnp.log(chosen_weight) - jnp.log(lax.optimization_barrier(jnp.sum(weights, axis=1))))
        norms.append(jnp.log(chosen_weight / CHI + epsilon))
        factor = lax.rsqrt(chosen_weight / CHI + epsilon)
        chosen = lax.optimization_barrier(jnp.sum(select[:, :, None] * displaced, axis=1))
        vectors = chosen.astype(jnp.bfloat16)
    return (jnp.stack(results), jnp.stack(norms))
```

```python
import functools
import math

import jax
import jax.numpy as jnp
from jax import lax
from jax.experimental import pallas as pl
from jax.experimental.pallas import tpu as pltpu
from jax.sharding import PartitionSpec as P

CUT = 4
EPS = 1e-06
ROWS = 16
MESH = pl.DeviceIdType.MESH


def displacement_table(cutoff):
    table = [[[0.0] * (2 * cutoff - 1) for _ in range(cutoff)] for _ in range(cutoff)]
    for row in range(cutoff):
        for col in range(cutoff):
            lower, upper = min(row, col), max(row, col)
            excess = upper - lower
            parity = 1.0 if row >= col else (-1.0) ** excess
            prefactor = math.sqrt(math.factorial(lower) / math.factorial(upper))
            for term in range(lower + 1):
                table[row][col][excess + 2 * term] += (
                    parity * prefactor * (-1.0) ** term * math.comb(upper, lower - term) / math.factorial(term)
                )
    return table


def ring_order(nz):
    return sorted(range(nz), key=lambda d: (min(d, nz - d), d))


def kernel(dims, left, tensor, disp, count, modes, out_ll, out_ln,
           tv, recv, sendv, acc_ref, fac, rows, rrow, prow, ak, aks, gm, gs,
           t_sem, near_sem, far_sem, fnear_sem, ffar_sem, row_sem, ak_sem, p_sem,
           vsend, fsend, rsend, lsend, aksend, psend):
    nsec, nz, blocks, width = dims
    nb = 2 * nz
    chi = nb * width
    order = ring_order(nz)
    far = max(1, (3 * nz) // 8)
    near = nz - far
    s, b = lax.axis_index("sec"), lax.axis_index("bond")
    z, c = b // 2, lax.rem(b, 2)
    sib = 2 * z + 1 - c
    not_first, not_last = s > 0, s < nsec - 1

    def rows_of(q):
        p, other = q % nz, q // nz
        core = c if other == 0 else 1 - c
        return (2 * lax.rem(z + nz - order[p], nz) + core) * width

    loads = []
    for q in range(nb):
        start = pl.multiple_of(rows_of(q), width)
        load = pltpu.make_async_copy(tensor.at[pl.ds(start, width), :], tv.at[q], t_sem.at[q])
        load.start()
        loads.append(load)

    barrier = pltpu.get_barrier_semaphore()

    def greet(sec, bond):
        pl.semaphore_signal(barrier, inc=1, device_id=(sec, bond), device_id_type=MESH)

    def greet_bond(q, carry):
        @pl.when(q != b)
        def _():
            greet(s, q)

        @pl.when(not_last)
        def _():
            greet(s + 1, q)

        @pl.when(not_first)
        def _():
            greet(s - 1, q)

        return carry

    def greet_sec(j, carry):
        @pl.when((j < s - 1) | (j > s + 1))
        def _():
            greet(j, b)

        return carry

    lax.fori_loop(0, nb, greet_bond, 0)
    lax.fori_loop(0, nsec, greet_sec, 0)
    sides = not_first.astype(jnp.int32) + not_last.astype(jnp.int32)

    lane_mode = lax.broadcasted_iota(jnp.int32, disp.shape, 1)

    def pick(j, carry):
        mine = lane_mode == modes[j]
        a = jnp.sum(jnp.where(mine, disp[...], 0.0), axis=1, keepdims=True)
        k = jnp.sum(jnp.where(mine, count[...].astype(jnp.float32), 0.0), axis=1, keepdims=True)
        aks[j, 0] = jnp.broadcast_to(a, (8, 128))
        aks[j, 1] = jnp.broadcast_to(k, (8, 128))
        return carry

    lax.fori_loop(0, nsec, pick, 0)
    ak[s] = aks[s]

    pl.semaphore_wait(barrier, nb - 1 + nb * sides + (nsec - 1 - sides))

    def target(d):
        return 2 * lax.rem(z + d, nz) + c

    def piece_sem(p, t):
        return near_sem.at[t] if p < near else far_sem.at[t]

    def send_pieces(src, t, sec, sem, local):
        for p in reversed(range(nz)):
            if p == 0 and local:
                pltpu.make_async_copy(src, recv.at[t, 0], near_sem.at[t]).start()
                continue
            pltpu.make_async_remote_copy(
                src_ref=src, dst_ref=recv.at[t, p], send_sem=sem, recv_sem=piece_sem(p, t),
                device_id=(sec, target(order[p])), device_id_type=MESH,
            ).start()

    @pl.when(s == 0)
    def _():
        def opening(t, carry):
            send_pieces(left.at[t], t, s, lsend, True)
            return carry

        lax.fori_loop(0, blocks, opening, 0)

    def share(i, carry):
        j = lax.rem(s + 1 + i, nsec)
        pltpu.make_async_remote_copy(
            src_ref=aks.at[j], dst_ref=ak.at[s], send_sem=aksend, recv_sem=ak_sem,
            device_id=(j, b), device_id_type=MESH,
        ).start()
        return carry

    lax.fori_loop(0, nsec - 1, share, 0)

    def wait_bytes(ref, sem):
        pltpu.make_async_copy(ref, ref, sem).wait()

    wait_bytes(ak.at[pl.ds(0, nsec - 1)], ak_sem)

    table = displacement_table(CUT)

    def matrices(t, carry):
        both = ak[pl.ds(2 * t, 2)]
        a = both[:, 0].reshape(ROWS, 128)
        k = both[:, 1].reshape(ROWS, 128)
        power = [None, a]
        for _ in range(2 * CUT - 3):
            power.append(power[-1] * a)
        envelope = jnp.exp(-0.5 * a * a)
        full = [[None] * CUT for _ in range(CUT)]
        for m in range(CUT):
            for n in range(CUT):
                if m < n:
                    continue
                poly = None
                for degree, value in enumerate(table[m][n]):
                    if value != 0.0:
                        term = value if degree == 0 else value * power[degree]
                        poly = term if poly is None else poly + term
                full[m][n] = envelope * poly
                full[n][m] = full[m][n] if (m - n) % 2 == 0 else -full[m][n]
        for m in range(CUT):
            for n in range(CUT):
                gm[t, m * CUT + n] = full[m][n]
        for n in range(CUT):
            g = full[CUT - 1][n]
            for m in reversed(range(CUT - 1)):
                g = jnp.where(k == float(m), full[m][n], g)
            gs[t, n] = g
        return carry

    lax.fori_loop(0, blocks, matrices, 0)

    lane = lax.broadcasted_iota(jnp.int32, (ROWS, 128), 1)
    sample = lax.broadcasted_iota(jnp.int32, (ROWS, 128), 0)

    def dots(acc, t, first, last):
        for q in range(first, last):
            part = jnp.dot(recv[t, q], tv[q], preferred_element_type=jnp.float32)
            acc = part if acc is None else acc + part
        return acc

    def forward(t, first, last, sem):
        pltpu.make_async_remote_copy(
            src_ref=recv.at[t, pl.ds(first, last - first)], dst_ref=recv.at[t, pl.ds(nz + first, last - first)],
            send_sem=fsend, recv_sem=sem.at[t], device_id=(s, sib), device_id_type=MESH,
        ).start()

    def near_part(t):
        wait_bytes(recv.at[t, pl.ds(0, near)], near_sem.at[t])
        forward(t, 0, near, fnear_sem)
        acc = dots(None, t, 0, near)
        wait_bytes(recv.at[t, pl.ds(nz, near)], fnear_sem.at[t])
        acc_ref[...] = dots(acc, t, nz, nz + near)

    fac[...] = jnp.ones_like(fac)
    for load in loads:
        load.wait()
    near_part(0)

    def one_block(t, carry):
        wait_bytes(recv.at[t, pl.ds(near, far)], far_sem.at[t])
        forward(t, near, nz, ffar_sem)
        acc = dots(acc_ref[...], t, near, nz)

        @pl.when(t < blocks - 1)
        def _():
            near_part(t + 1)

        @pl.when(not_first)
        def _():
            wait_bytes(rrow.at[t], row_sem.at[t])
            total = jnp.sum(rrow[t], axis=0)
            weight = jnp.sum(jnp.where(lane == CUT * ROWS + sample, total, 0.0), axis=1, keepdims=True)
            fac[...] = jnp.broadcast_to(lax.rsqrt(weight * (1.0 / chi) + EPS), (ROWS, 128))

        wait_bytes(recv.at[t, pl.ds(nz + near, far)], ffar_sem.at[t])
        acc = dots(acc, t, nz + near, nb) * fac[:, :1]
        proj = [[acc[:, n * width + h * 128:n * width + (h + 1) * 128] for h in range(width // 128)]
                for n in range(CUT)]

        def mix(g):
            return [sum(g[n] * proj[n][h] for n in range(CUT)) for h in range(width // 128)]

        chosen = mix([gs[t, n] for n in range(CUT)])
        sendv[t] = jnp.concatenate(chosen, axis=1).astype(jnp.bfloat16)

        @pl.when(not_last)
        def _():
            send_pieces(sendv.at[t], t, s + 1, vsend, False)

        packed = jnp.zeros((ROWS, 128), jnp.float32)
        k = jnp.concatenate([ak[2 * t, 1], ak[2 * t + 1, 1]], axis=0)
        picked = None
        for m in range(CUT):
            level = mix([gm[t, m * CUT + n] for n in range(CUT)])
            w = jnp.sum(sum(x * x for x in level), axis=1, keepdims=True)
            w = jnp.broadcast_to(w, (ROWS, 128))
            packed = jnp.where(lane == m * ROWS + sample, w, packed)
            picked = w if picked is None else jnp.where(k == float(m), w, picked)
        packed = jnp.where(lane == CUT * ROWS + sample, picked, packed)
        rows[t] = jnp.sum(packed, axis=0, keepdims=True)

        @pl.when(not_last)
        def _():
            for p in reversed(range(nz)):
                for other in range(2):
                    pltpu.make_async_remote_copy(
                        src_ref=rows.at[t], dst_ref=rrow.at[t, other * nz + p], send_sem=rsend, recv_sem=row_sem.at[t],
                        device_id=(s + 1, 2 * lax.rem(z + order[p], nz) + (c if other == 0 else 1 - c)),
                        device_id_type=MESH,
                    ).start()

        return carry

    lax.fori_loop(0, blocks, one_block, 0)

    prow[b] = rows[...]

    def spread(i, carry):
        q = lax.rem(b + 1 + i, nb)
        pltpu.make_async_remote_copy(
            src_ref=rows, dst_ref=prow.at[b], send_sem=psend, recv_sem=p_sem,
            device_id=(s, q), device_id_type=MESH,
        ).start()
        return carry

    lax.fori_loop(0, nb - 1, spread, 0)

    @pl.when(s == 0)
    def _():
        wait_bytes(recv.at[:, pl.ds(1, nz - 1)], lsend)

    @pl.when(not_last)
    def _():
        wait_bytes(recv.at[:, pl.ds(0, nz)], vsend)
        wait_bytes(rrow, rsend)

    wait_bytes(recv.at[:, pl.ds(0, nz)], fsend)
    wait_bytes(aks.at[pl.ds(0, nsec - 1)], aksend)
    wait_bytes(prow.at[pl.ds(0, nb - 1)], p_sem)
    wait_bytes(prow.at[pl.ds(0, nb - 1)], psend)

    samples = blocks * ROWS
    out_lane = lax.broadcasted_iota(jnp.int32, (ROWS, samples), 1)
    out_sample = lax.broadcasted_iota(jnp.int32, (ROWS, samples), 0)
    in_level = (lane < CUT * ROWS) & (lax.rem(lane, ROWS) == sample)

    def finish(t, carry):
        ll, ln = carry
        total = jnp.sum(prow[:, t], axis=0)
        chosen = jnp.sum(jnp.where(lane == CUT * ROWS + sample, total, 0.0), axis=1, keepdims=True)
        every = jnp.sum(jnp.where(in_level, total, 0.0), axis=1, keepdims=True)
        here = out_lane == t * ROWS + out_sample
        ll = jnp.where(here, jnp.log(chosen) - jnp.log(every), ll)
        ln = jnp.where(here, jnp.log(chosen * (1.0 / chi) + EPS), ln)
        return ll, ln

    zero = jnp.zeros((ROWS, samples), jnp.float32)
    ll, ln = lax.fori_loop(0, blocks, finish, (zero, zero))
    out_ll[...] = jnp.sum(ll, axis=0, keepdims=True)
    out_ln[...] = jnp.sum(ln, axis=0, keepdims=True)


def local(left_vectors, site_tensors, displacement, photon_counts, mode_order):
    nsec, nb = lax.axis_size("sec"), lax.axis_size("bond")
    samples, width = left_vectors.shape
    blocks = samples // ROWS
    matrix = site_tensors.reshape(nb * width, CUT * width)
    left = left_vectors.reshape(blocks, ROWS, width)
    vmem = pl.BlockSpec(memory_space=pltpu.VMEM)
    dma = pltpu.SemaphoreType.DMA
    return pl.pallas_call(
        functools.partial(kernel, (nsec, nb // 2, blocks, width)),
        out_shape=[jax.ShapeDtypeStruct((1, samples), jnp.float32)] * 2,
        in_specs=[vmem, pl.BlockSpec(memory_space=pl.ANY), vmem, vmem, pl.BlockSpec(memory_space=pltpu.SMEM)],
        out_specs=[vmem, vmem],
        scratch_shapes=[
            pltpu.VMEM((nb, width, CUT * width), jnp.bfloat16),
            pltpu.VMEM((blocks, nb, ROWS, width), jnp.bfloat16),
            pltpu.VMEM((blocks, ROWS, width), jnp.bfloat16),
            pltpu.VMEM((ROWS, CUT * width), jnp.float32),
            pltpu.VMEM((ROWS, 128), jnp.float32),
            pltpu.VMEM((blocks, 1, 128), jnp.float32),
            pltpu.VMEM((blocks, nb, 1, 128), jnp.float32),
            pltpu.VMEM((nb, blocks, 1, 128), jnp.float32),
            pltpu.VMEM((nsec, 2, 8, 128), jnp.float32),
            pltpu.VMEM((nsec, 2, 8, 128), jnp.float32),
            pltpu.VMEM((blocks, CUT * CUT, ROWS, 128), jnp.float32),
            pltpu.VMEM((blocks, CUT, ROWS, 128), jnp.float32),
            dma((nb,)),
            dma((blocks,)),
            dma((blocks,)),
            dma((blocks,)),
            dma((blocks,)),
            dma((blocks,)),
            dma, dma, dma, dma, dma, dma, dma, dma,
        ],
        compiler_params=pltpu.CompilerParams(
            collective_id=0, has_side_effects=True, vmem_limit_bytes=40 * 2**20
        ),
        cost_estimate=pl.CostEstimate(
            flops=2 * samples * matrix.size, bytes_accessed=2 * matrix.size, transcendentals=samples * 128
        ),
        name="chain",
    )(left, matrix, displacement, photon_counts, mode_order)


def solution(mesh):
    placed = (P(None, "bond"), P("sec", None, None, "bond"), P("sec", None), P("sec", None), P())
    return jax.shard_map(
        local,
        mesh=mesh,
        in_specs=placed,
        out_specs=(P("sec", None), P("sec", None)),
        check_vma=False,
    )
```

```python
import functools
import math

import jax
import jax.numpy as jnp
from jax import lax
from jax.experimental import pallas as pl
from jax.experimental.pallas import tpu as pltpu
from jax.sharding import PartitionSpec as P

CUT = 4
EPS = 1e-06
ROWS = 16
MESH = pl.DeviceIdType.MESH


def displacement_table(cutoff):
    table = [[[0.0] * (2 * cutoff - 1) for _ in range(cutoff)] for _ in range(cutoff)]
    for row in range(cutoff):
        for col in range(cutoff):
            lower, upper = min(row, col), max(row, col)
            excess = upper - lower
            parity = 1.0 if row >= col else (-1.0) ** excess
            prefactor = math.sqrt(math.factorial(lower) / math.factorial(upper))
            for term in range(lower + 1):
                table[row][col][excess + 2 * term] += (
                    parity * prefactor * (-1.0) ** term * math.comb(upper, lower - term) / math.factorial(term)
                )
    return table


def ring_order(nz):
    return sorted(range(nz), key=lambda d: (min(d, nz - d), d))


def kernel(dims, left, tensor, disp, count, modes, out_ll, out_ln,
           tv, recv, sendv, acc_ref, nrm, rows, prow, ak, aks, gm, gs,
           t_sem, near_sem, far_sem, fnear_sem, ak_sem, p_sem,
           vsend, fsend, lsend, aksend, psend):
    nsec, nz, blocks, width = dims
    nb = 2 * nz
    chi = nb * width
    order = ring_order(nz)
    far = max(1, (3 * nz) // 8)
    near = nz - far
    s, b = lax.axis_index("sec"), lax.axis_index("bond")
    z, c = b // 2, lax.rem(b, 2)
    sib = 2 * z + 1 - c
    not_first, not_last = s > 0, s < nsec - 1

    def rows_of(q):
        p, other = q % nz, q // nz
        core = c if other == 0 else 1 - c
        return (2 * lax.rem(z + nz - order[p], nz) + core) * width

    loads = []
    for q in range(nb):
        start = pl.multiple_of(rows_of(q), width)
        load = pltpu.make_async_copy(tensor.at[pl.ds(start, width), :], tv.at[q], t_sem.at[q])
        load.start()
        loads.append(load)

    barrier = pltpu.get_barrier_semaphore()

    def greet(sec, bond):
        pl.semaphore_signal(barrier, inc=1, device_id=(sec, bond), device_id_type=MESH)

    def target(d, other):
        return 2 * lax.rem(z + d, nz) + (1 - c if other else c)

    fan = [(p, other) for p in reversed(range(nz)) for other in range(2) if p >= near or not other]

    def greet_bond(i, carry):
        greet(s, lax.rem(b + 1 + i, nb))
        return carry

    @pl.when(not_last)
    def _():
        for p, other in fan:
            greet(s + 1, target(order[p], other))

    @pl.when(not_first)
    def _():
        for p, other in fan:
            greet(s - 1, target(nz - order[p], other))

    def greet_sec(j, carry):
        @pl.when((j < s - 1) | (j > s + 1))
        def _():
            greet(j, b)

        return carry

    lax.fori_loop(0, nb - 1, greet_bond, 0)
    lax.fori_loop(0, nsec, greet_sec, 0)
    sides = not_first.astype(jnp.int32) + not_last.astype(jnp.int32)

    lane_mode = lax.broadcasted_iota(jnp.int32, disp.shape, 1)

    def pick(j, carry):
        mine = lane_mode == modes[j]
        a = jnp.sum(jnp.where(mine, disp[...], 0.0), axis=1, keepdims=True)
        k = jnp.sum(jnp.where(mine, count[...].astype(jnp.float32), 0.0), axis=1, keepdims=True)
        aks[j, 0] = jnp.broadcast_to(a, (8, 128))
        aks[j, 1] = jnp.broadcast_to(k, (8, 128))
        return carry

    lax.fori_loop(0, nsec, pick, 0)
    ak[s] = aks[s]

    pl.semaphore_wait(barrier, nb - 1 + len(fan) * sides + (nsec - 1 - sides))

    def send_pieces(src, t, sec, sem, local):
        for p, other in fan:
            slot = other * nz + p
            if slot == 0 and local:
                pltpu.make_async_copy(src, recv.at[t, 0], near_sem.at[t]).start()
                continue
            pltpu.make_async_remote_copy(
                src_ref=src, dst_ref=recv.at[t, slot], send_sem=sem,
                recv_sem=near_sem.at[t] if p < near else far_sem.at[t],
                device_id=(sec, target(order[p], other)), device_id_type=MESH,
            ).start()

    @pl.when(s == 0)
    def _():
        def opening(t, carry):
            send_pieces(left.at[t], t, s, lsend, True)
            return carry

        lax.fori_loop(0, blocks, opening, 0)

    def share(i, carry):
        j = lax.rem(s + 1 + i, nsec)
        pltpu.make_async_remote_copy(
            src_ref=aks.at[j], dst_ref=ak.at[s], send_sem=aksend, recv_sem=ak_sem,
            device_id=(j, b), device_id_type=MESH,
        ).start()
        return carry

    lax.fori_loop(0, nsec - 1, share, 0)

    def wait_bytes(ref, sem):
        pltpu.make_async_copy(ref, ref, sem).wait()

    wait_bytes(ak.at[pl.ds(0, nsec - 1)], ak_sem)

    table = displacement_table(CUT)

    def matrices(t, carry):
        both = ak[pl.ds(2 * t, 2)]
        a = both[:, 0].reshape(ROWS, 128)
        k = both[:, 1].reshape(ROWS, 128)
        power = [None, a]
        for _ in range(2 * CUT - 3):
            power.append(power[-1] * a)
        envelope = jnp.exp(-0.5 * a * a)
        full = [[None] * CUT for _ in range(CUT)]
        for m in range(CUT):
            for n in range(CUT):
                if m < n:
                    continue
                poly = None
                for degree, value in enumerate(table[m][n]):
                    if value != 0.0:
                        term = value if degree == 0 else value * power[degree]
                        poly = term if poly is None else poly + term
                full[m][n] = envelope * poly
                full[n][m] = full[m][n] if (m - n) % 2 == 0 else -full[m][n]
        for m in range(CUT):
            for n in range(CUT):
                gm[t, m * CUT + n] = full[m][n]
        for n in range(CUT):
            g = full[CUT - 1][n]
            for m in reversed(range(CUT - 1)):
                g = jnp.where(k == float(m), full[m][n], g)
            gs[t, n] = g
        return carry

    lax.fori_loop(0, blocks, matrices, 0)

    lane = lax.broadcasted_iota(jnp.int32, (ROWS, 128), 1)
    sample = lax.broadcasted_iota(jnp.int32, (ROWS, 128), 0)

    def dots(acc, squares, t, first, last):
        for q in range(first, last):
            piece = recv[t, q]
            part = jnp.dot(piece, tv[q], preferred_element_type=jnp.float32)
            acc = part if acc is None else acc + part
            wide = piece.astype(jnp.float32)
            for h in range(width // 128):
                half = wide[:, h * 128:(h + 1) * 128]
                squares = half * half if squares is None else squares + half * half
        return acc, squares

    def near_part(t):
        wait_bytes(recv.at[t, pl.ds(0, near)], near_sem.at[t])
        pltpu.make_async_remote_copy(
            src_ref=recv.at[t, pl.ds(0, near)], dst_ref=recv.at[t, pl.ds(nz, near)],
            send_sem=fsend, recv_sem=fnear_sem.at[t], device_id=(s, sib), device_id_type=MESH,
        ).start()
        acc, squares = dots(None, None, t, 0, near)
        wait_bytes(recv.at[t, pl.ds(nz, near)], fnear_sem.at[t])
        acc_ref[...], nrm[...] = dots(acc, squares, t, nz, nz + near)

    for load in loads:
        load.wait()
    near_part(0)

    def one_block(t, carry):
        wait_bytes(recv.at[t, pl.ds(0, 2 * far)], far_sem.at[t])
        acc, squares = dots(acc_ref[...], nrm[...], t, near, nz)
        acc, squares = dots(acc, squares, t, nz + near, nb)
        weight = jnp.sum(squares, axis=1, keepdims=True)
        acc = acc * jnp.where(not_first, lax.rsqrt(weight * (1.0 / chi) + EPS), 1.0)
        proj = [[acc[:, n * width + h * 128:n * width + (h + 1) * 128] for h in range(width // 128)]
                for n in range(CUT)]

        def mix(g):
            return [sum(g[n] * proj[n][h] for n in range(CUT)) for h in range(width // 128)]

        chosen = mix([gs[t, n] for n in range(CUT)])
        sendv[t] = jnp.concatenate(chosen, axis=1).astype(jnp.bfloat16)

        @pl.when(not_last)
        def _():
            send_pieces(sendv.at[t], t, s + 1, vsend, False)

        packed = jnp.zeros((ROWS, 128), jnp.float32)
        k = jnp.concatenate([ak[2 * t, 1], ak[2 * t + 1, 1]], axis=0)
        picked = None
        for m in range(CUT):
            level = mix([gm[t, m * CUT + n] for n in range(CUT)])
            w = jnp.sum(sum(x * x for x in level), axis=1, keepdims=True)
            w = jnp.broadcast_to(w, (ROWS, 128))
            packed = jnp.where(lane == m * ROWS + sample, w, packed)
            picked = w if picked is None else jnp.where(k == float(m), w, picked)
        packed = jnp.where(lane == CUT * ROWS + sample, picked, packed)
        rows[t] = jnp.sum(packed, axis=0, keepdims=True)

        @pl.when(t < blocks - 1)
        def _():
            near_part(t + 1)

        return carry

    lax.fori_loop(0, blocks, one_block, 0)

    prow[b] = rows[...]

    def spread(i, carry):
        q = lax.rem(b + 1 + i, nb)
        pltpu.make_async_remote_copy(
            src_ref=rows, dst_ref=prow.at[b], send_sem=psend, recv_sem=p_sem,
            device_id=(s, q), device_id_type=MESH,
        ).start()
        return carry

    lax.fori_loop(0, nb - 1, spread, 0)

    @pl.when(s == 0)
    def _():
        wait_bytes(recv.at[:, pl.ds(1, len(fan) - 1)], lsend)

    @pl.when(not_last)
    def _():
        wait_bytes(recv.at[:, pl.ds(0, len(fan))], vsend)

    wait_bytes(recv.at[:, pl.ds(0, near)], fsend)
    wait_bytes(aks.at[pl.ds(0, nsec - 1)], aksend)
    wait_bytes(prow.at[pl.ds(0, nb - 1)], p_sem)
    wait_bytes(prow.at[pl.ds(0, nb - 1)], psend)

    samples = blocks * ROWS
    out_lane = lax.broadcasted_iota(jnp.int32, (ROWS, samples), 1)
    out_sample = lax.broadcasted_iota(jnp.int32, (ROWS, samples), 0)
    in_level = (lane < CUT * ROWS) & (lax.rem(lane, ROWS) == sample)

    def finish(t, carry):
        ll, ln = carry
        total = jnp.sum(prow[:, t], axis=0)
        chosen = jnp.sum(jnp.where(lane == CUT * ROWS + sample, total, 0.0), axis=1, keepdims=True)
        every = jnp.sum(jnp.where(in_level, total, 0.0), axis=1, keepdims=True)
        here = out_lane == t * ROWS + out_sample
        ll = jnp.where(here, jnp.log(chosen) - jnp.log(every), ll)
        ln = jnp.where(here, jnp.log(chosen * (1.0 / chi) + EPS), ln)
        return ll, ln

    zero = jnp.zeros((ROWS, samples), jnp.float32)
    ll, ln = lax.fori_loop(0, blocks, finish, (zero, zero))
    out_ll[...] = jnp.sum(ll, axis=0, keepdims=True)
    out_ln[...] = jnp.sum(ln, axis=0, keepdims=True)


def local(left_vectors, site_tensors, displacement, photon_counts, mode_order):
    nsec, nb = lax.axis_size("sec"), lax.axis_size("bond")
    samples, width = left_vectors.shape
    blocks = samples // ROWS
    matrix = site_tensors.reshape(nb * width, CUT * width)
    left = left_vectors.reshape(blocks, ROWS, width)
    vmem = pl.BlockSpec(memory_space=pltpu.VMEM)
    dma = pltpu.SemaphoreType.DMA
    return pl.pallas_call(
        functools.partial(kernel, (nsec, nb // 2, blocks, width)),
        out_shape=[jax.ShapeDtypeStruct((1, samples), jnp.float32)] * 2,
        in_specs=[vmem, pl.BlockSpec(memory_space=pl.ANY), vmem, vmem, pl.BlockSpec(memory_space=pltpu.SMEM)],
        out_specs=[vmem, vmem],
        scratch_shapes=[
            pltpu.VMEM((nb, width, CUT * width), jnp.bfloat16),
            pltpu.VMEM((blocks, nb, ROWS, width), jnp.bfloat16),
            pltpu.VMEM((blocks, ROWS, width), jnp.bfloat16),
            pltpu.VMEM((ROWS, CUT * width), jnp.float32),
            pltpu.VMEM((ROWS, 128), jnp.float32),
            pltpu.VMEM((blocks, 1, 128), jnp.float32),
            pltpu.VMEM((nb, blocks, 1, 128), jnp.float32),
            pltpu.VMEM((nsec, 2, 8, 128), jnp.float32),
            pltpu.VMEM((nsec, 2, 8, 128), jnp.float32),
            pltpu.VMEM((blocks, CUT * CUT, ROWS, 128), jnp.float32),
            pltpu.VMEM((blocks, CUT, ROWS, 128), jnp.float32),
            dma((nb,)),
            dma((blocks,)),
            dma((blocks,)),
            dma((blocks,)),
            dma, dma, dma, dma, dma, dma, dma,
        ],
        compiler_params=pltpu.CompilerParams(
            collective_id=0, has_side_effects=True, vmem_limit_bytes=60 * 2**20
        ),
        cost_estimate=pl.CostEstimate(
            flops=2 * samples * matrix.size, bytes_accessed=2 * matrix.size, transcendentals=samples * 128
        ),
        name="chain",
    )(left, matrix, displacement, photon_counts, mode_order)


def solution(mesh):
    placed = (P(None, "bond"), P("sec", None, None, "bond"), P("sec", None), P("sec", None), P())
    return jax.shard_map(
        local,
        mesh=mesh,
        in_specs=placed,
        out_specs=(P("sec", None), P("sec", None)),
        check_vma=False,
    )
```
